32 devices in a mesh: row: 4 (over y, x), col: 8 (over z, core).
Axes of the slice: x: 2, y: 2, z: 4, core: 2. Of those that a mesh axis runs over, the one named last changes fastest.
Arguments:
- playlist_items: bfloat16 [4096, 8192], P('row', 'col'), may hold values from -6 to 6
- tile_live: int32 [4, 8], P('row', 'col'), may hold values 0 or 1
- playlist_weights: int32 [4096], P('row'), may hold values from 1 to 8
Outputs:
- cooccur: float32 [4096, 8192], P('row', 'col')
The draws below stay inside these ranges and needn't reach their ends.
All inputs are finite; a program needn't handle non-finite values. No bound on the sum of `tile_live` on one device may be relied on, other than what follows from the above.
Results may differ from the reference program's by a relative error of at most 0.002.
Values may be sent and summed in bfloat16 or wider, within the bound.
No kernel may reach another device: no remote copies, remote signals or barrier semaphores. Data moves between devices by JAX's collectives and lax.ppermute only.
A program may use at most 128 MiB of HBM per device.

```python
import jax
import jax.numpy as jnp
from jax import lax

TILE = 1024
PBLK = 4
IBLK = 8
PLAYLISTS = 4096
ITEMS = 8192
BAND = 4096


def touch_ends(array, stream_key, least, high):
    longest = array.shape.index(max(array.shape))
    spots = []
    for shift in (0, 1):
        where = [jax.random.randint(jax.random.fold_in(stream_key, axis), (), 0, length) for axis, length in enumerate(array.shape)]
        where[longest] = (where[longest] + shift) % array.shape[longest]
        spots.append(tuple(where))
    return array.at[spots[0]].set(least).at[spots[1]].set(high)


def steps_of(rng, dims, pieces, least, top_value):
    level, own = 1.0, jax.random.fold_in(rng, 6)
    for axis_at, parts in pieces:
        steps = jnp.exp(jax.random.uniform(jax.random.fold_in(own, axis_at), (parts,), jnp.float32, least / len(pieces), top_value / len(pieces)))
        level = level * jnp.repeat(steps, dims[axis_at] // parts).reshape([-1 if axis == axis_at else 1 for axis in range(len(dims))])
    return level


def scatter_about(rng, shape, width, limit, pieces=(), held_as=jnp.bfloat16):
    array = width * jax.random.normal(rng, shape, jnp.float32)
    if pieces:
        array = array * steps_of(rng, shape, pieces, -0.22, 0.18)
    return jnp.clip(array, -limit, limit).astype(held_as)


def setup_inputs(seed: int = 0) -> dict:
    key_list = jax.random.split(jax.random.key(seed), 4)
    return {
        "playlist_items": scatter_about(key_list[0], (PLAYLISTS, ITEMS), 1.0, 6.0, ((0, 4), (1, 8))),
        "tile_live": touch_ends((jax.random.randint(key_list[1], (PBLK, IBLK), 0, 4) < 3).astype(jnp.int32), jax.random.fold_in(key_list[1], 1), 0, 1),
        "playlist_weights": touch_ends(jax.random.randint(key_list[2], (PLAYLISTS,), 1, 9), jax.random.fold_in(key_list[2], 1), 1, 8).astype(jnp.int32),
    }


def reference(playlist_items, tile_live, playlist_weights):
    tiled = playlist_items.reshape(PBLK, TILE, IBLK, TILE)
    keep = tile_live[:, None, :, None] > 0
    masked = jnp.where(keep, tiled, jnp.zeros_like(tiled)).reshape(PLAYLISTS, ITEMS)
    scaled = (playlist_weights[:, None].astype(jnp.float32) * masked.astype(jnp.float32)).astype(jnp.bfloat16)
    band_part = masked[:, :BAND]
    summed = lax.dot_general(band_part, scaled, (((0,), (0,)), ((), ())), preferred_element_type=jnp.float32)
    return summed / jnp.float32(PLAYLISTS)
```

```python
import jax
import jax.numpy as jnp
from jax import lax
from jax.sharding import PartitionSpec as P


def broadcast(x, axis, root):
    mine = lax.axis_index(axis) == root
    return lax.psum(jnp.where(mine, x, jnp.zeros_like(x)), axis)


def per_device_general(playlist_items, tile_live, playlist_weights):
    masked = jnp.where(tile_live[0, 0] > 0, playlist_items, jnp.zeros_like(playlist_items))
    column = lax.all_gather(masked, "row", axis=0, tiled=True)
    weights = lax.all_gather(playlist_weights, "row", axis=0, tiled=True)
    scaled = (weights[:, None].astype(jnp.float32) * column.astype(jnp.float32)).astype(jnp.bfloat16)
    band = broadcast(column, "col", lax.axis_index("row"))
    summed = lax.dot_general(band, scaled, (((0,), (0,)), ((), ())), preferred_element_type=jnp.float32)
    return summed / jnp.float32(column.shape[0])


def pairs(*rules):
    out = []
    for n in range(32):
        at = (n >> 4, (n >> 3) & 1, (n >> 1) & 3, n & 1)
        for rule in rules:
            to = rule(*at)
            if to is not None:
                out.append((n, to[0] * 16 + to[1] * 8 + to[2] * 2 + to[3]))
    return out


def across(y, x, z, k):
    return (y, k, z, x) if z < 2 else None


def one_up(y, x, z, k):
    return (y, x, z + 1, k) if z < 2 else None


def one_to_two(y, x, z, k):
    return (y, x, 2, k) if z == 1 else None


def two_to_three(y, x, z, k):
    return (y, x, 3, k) if z == 2 else None


def one_to_none(y, x, z, k):
    return (y, x, 0, k) if z == 1 else None


ACROSS, ONE_UP, ONE_TO_TWO = pairs(across), pairs(one_up), pairs(one_to_two)
OUTWARD, TWO_TO_THREE = pairs(two_to_three, one_to_none), pairs(two_to_three)
SWAP_X = pairs(lambda y, x, z, k: (y, 1 - x, z, k))
SWAP_Y = pairs(lambda y, x, z, k: (1 - y, x, z, k))
SWAP_Z = pairs(lambda y, x, z, k: (y, x, z ^ 1, k))
CORES = pairs(lambda y, x, z, k: (y, x, z, 1 - k))


def send(value, perm):
    return lax.ppermute(value, ("row", "col"), perm)


def after(value, *others):
    return lax.optimization_barrier((value,) + others)[0]


def cuts_of(cols):
    unit = cols // 8
    at, out = 0, []
    for width in (1, 3, 3, 1):
        out.append((at, at + width * unit))
        at += width * unit
    return out


def per_device(playlist_items, tile_live, playlist_weights):
    rows, cols = playlist_items.shape
    r, c = lax.axis_index("row"), lax.axis_index("col")
    y, x, z, k = r // 2, r % 2, c // 2, c % 2
    live = tile_live[0, 0] > 0
    cuts = cuts_of(cols)

    def keep(block):
        return jnp.where(live, block, jnp.zeros_like(block))

    n = len(cuts)
    pieces = [keep(playlist_items[:, lo:hi]) for lo, hi in cuts]
    own = keep(playlist_items)
    w_near = send(playlist_weights, SWAP_X)
    base, up, up2, out, out2 = [], [], [], [], []
    for j in range(n):
        base.append(send(after(pieces[j], base[j - 2]) if j >= 2 else after(pieces[j], w_near), ACROSS))
    near = send(after(own, w_near, *base), SWAP_X)
    for j in range(n):
        up.append(send(after(base[j], up[j - 1]) if j >= 2 else base[j], ONE_UP))
        up2.append(send(after(up[j], up2[j - 1]) if j >= 1 else up[j], ONE_TO_TWO))
        out.append(send(jnp.where(z == 1, base[j], up[j]), OUTWARD))
        out2.append(send(up2[j], TWO_TO_THREE))

    def scale(block, weight):
        return (weight[:, None].astype(jnp.float32) * block.astype(jnp.float32)).astype(jnp.bfloat16)

    def dot(lhs, rhs):
        return lax.dot_general(lhs, rhs, (((0,), (0,)), ((), ())), preferred_element_type=jnp.float32)

    here, there = scale(own, playlist_weights), scale(near, w_near)
    by_mine, by_their = jnp.where(k == x, here, there), jnp.where(k == x, there, here)
    outs, fars = [], []
    for j, (lo, hi) in enumerate(cuts):
        high = jnp.where(z == 1, base[j], jnp.where(z == 2, up[j], out[j]))
        low = jnp.where(z == 0, base[j], jnp.where(z == 1, up[j], up2[j] + out2[j]))
        mine = jnp.concatenate([jnp.where(y == 1, high, low), jnp.where(y == 1, low, high)], 1)
        if j >= 2:
            mine = after(mine, fars[j - 2])
        their = send(mine, CORES)
        part = dot(mine, by_mine) + dot(their, by_their)
        far = send(part[hi - lo :].astype(jnp.bfloat16), SWAP_Y)
        fars.append(far)
        outs.append((part[: hi - lo] + far.astype(jnp.float32)) / jnp.float32(4 * rows))
    return jnp.concatenate(outs, 0)


def solution(mesh):
    tuned = mesh.shape["row"] == 4 and mesh.shape["col"] == 8
    return jax.shard_map(
        per_device if tuned else per_device_general,
        mesh=mesh,
        in_specs=(P("row", "col"), P("row", "col"), P("row")),
        out_specs=P("row", "col"),
        check_vma=False,
    )
```

```python
import jax
import jax.numpy as jnp
from jax import lax
from jax.sharding import PartitionSpec as P


def broadcast(x, axis, root):
    mine = lax.axis_index(axis) == root
    return lax.psum(jnp.where(mine, x, jnp.zeros_like(x)), axis)


def per_device_general(playlist_items, tile_live, playlist_weights):
    masked = jnp.where(tile_live[0, 0] > 0, playlist_items, jnp.zeros_like(playlist_items))
    column = lax.all_gather(masked, "row", axis=0, tiled=True)
    weights = lax.all_gather(playlist_weights, "row", axis=0, tiled=True)
    scaled = (weights[:, None].astype(jnp.float32) * column.astype(jnp.float32)).astype(jnp.bfloat16)
    band = broadcast(column, "col", lax.axis_index("row"))
    summed = lax.dot_general(band, scaled, (((0,), (0,)), ((), ())), preferred_element_type=jnp.float32)
    return summed / jnp.float32(column.shape[0])


def pairs(*rules):
    out = []
    for n in range(32):
        at = (n >> 4, (n >> 3) & 1, (n >> 1) & 3, n & 1)
        for rule in rules:
            to = rule(*at)
            if to is not None:
                out.append((n, to[0] * 16 + to[1] * 8 + to[2] * 2 + to[3]))
    return out


def across(y, x, z, k):
    return (y, k, z, x) if z < 2 else None


def one_up(y, x, z, k):
    return (y, x, z + 1, k) if z < 2 else None


def one_to_two(y, x, z, k):
    return (y, x, 2, k) if z == 1 else None


def two_to_three(y, x, z, k):
    return (y, x, 3, k) if z == 2 else None


def one_to_none(y, x, z, k):
    return (y, x, 0, k) if z == 1 else None


ACROSS, ONE_UP, ONE_TO_TWO = pairs(across), pairs(one_up), pairs(one_to_two)
OUTWARD, TWO_TO_THREE = pairs(two_to_three, one_to_none), pairs(two_to_three)
SWAP_X = pairs(lambda y, x, z, k: (y, 1 - x, z, k))
SWAP_Y = pairs(lambda y, x, z, k: (1 - y, x, z, k))
SWAP_Z = pairs(lambda y, x, z, k: (y, x, z ^ 1, k))
CORES = pairs(lambda y, x, z, k: (y, x, z, 1 - k))


def send(value, perm):
    return lax.ppermute(value, ("row", "col"), perm)


def after(value, *others):
    return lax.optimization_barrier((value,) + others)[0]


def cuts_of(cols):
    unit = cols // 8
    at, out = 0, []
    for width in (2, 2, 2, 2):
        out.append((at, at + width * unit))
        at += width * unit
    return out


def per_device(playlist_items, tile_live, playlist_weights):
    rows, cols = playlist_items.shape
    r, c = lax.axis_index("row"), lax.axis_index("col")
    y, x, z, k = r // 2, r % 2, c // 2, c % 2
    live = tile_live[0, 0] > 0
    cuts = cuts_of(cols)

    def keep(block):
        return jnp.where(live, block, jnp.zeros_like(block))

    n = len(cuts)
    w_near = send(playlist_weights, SWAP_X)
    lead = 3
    base = [send(keep(playlist_items[:, lo:hi]), ACROSS) for lo, hi in cuts[:lead]]
    rest = cuts[lead][0]
    tail = send(after(keep(playlist_items[:, rest:]), w_near), ACROSS)
    base += [tail[:, lo - rest : hi - rest] for lo, hi in cuts[lead:]]
    own = keep(playlist_items)

    def scale(block, weight):
        return (weight[:, None].astype(jnp.float32) * block.astype(jnp.float32)).astype(jnp.bfloat16)

    def dot(lhs, rhs):
        return lax.dot_general(lhs, rhs, (((0,), (0,)), ((), ())), preferred_element_type=jnp.float32)

    order = [(0, 0), (1, 0)]
    for j in range(2, n):
        order += [(j - 2, 1), (j, 0)]
    order += [(n - 2, 1), (n - 1, 1)]
    up, out = {}, {}
    for i, (j, leg) in enumerate(order):
        value = up[j, 0] if leg else base[j]
        ties = [up[order[i - 3]]] if i >= 3 else []
        if i >= 3:
            ties.append(out[order[i - 3]])
        if i == 5:
            ties.append(near[0])
        up[j, leg] = send(after(value, *ties) if ties else value, ONE_TO_TWO if leg else ONE_UP)
        if i == 1:
            near = []
            for h in range(1):
                ties = [w_near, up[order[i]]] if h == 0 else [near[h - 1]]
                near.append(send(after(own[:, h * (cols // 1) : (h + 1) * (cols // 1)], *ties), SWAP_X))

        if leg:
            out[j, 1] = send(up[j, 1], TWO_TO_THREE)
        else:
            out[j, 0] = send(jnp.where(z == 1, base[j], up[j, 0]), OUTWARD)
    up, up2 = [up[j, 0] for j in range(n)], [up[j, 1] for j in range(n)]
    out, out2 = [out[j, 0] for j in range(n)], [out[j, 1] for j in range(n)]

    here, there = scale(own, playlist_weights), scale(jnp.concatenate(near, 1), w_near)
    by_mine, by_their = jnp.where(k == x, here, there), jnp.where(k == x, there, here)
    outs, fars = [], []
    for j, (lo, hi) in enumerate(cuts):
        high = jnp.where(z == 1, base[j], jnp.where(z == 2, up[j], out[j]))
        low = jnp.where(z == 0, base[j], jnp.where(z == 1, up[j], up2[j] + out2[j]))
        mine = jnp.concatenate([jnp.where(y == 1, high, low), jnp.where(y == 1, low, high)], 1)
        if j >= 2:
            mine = after(mine, fars[j - 2])
        their = send(mine, CORES)
        part = dot(mine, by_mine) + dot(their, by_their)
        far = send(part[hi - lo :].astype(jnp.bfloat16), SWAP_Y)
        fars.append(far)
        outs.append((part[: hi - lo] + far.astype(jnp.float32)) / jnp.float32(4 * rows))
    return jnp.concatenate(outs, 0)


def solution(mesh):
    tuned = mesh.shape["row"] == 4 and mesh.shape["col"] == 8
    return jax.shard_map(
        per_device if tuned else per_device_general,
        mesh=mesh,
        in_specs=(P("row", "col"), P("row", "col"), P("row")),
        out_specs=P("row", "col"),
        check_vma=False,
    )
```

```python
import jax
import jax.numpy as jnp
from jax import lax
from jax.sharding import PartitionSpec as P


def broadcast(x, axis, root):
    mine = lax.axis_index(axis) == root
    return lax.psum(jnp.where(mine, x, jnp.zeros_like(x)), axis)


def per_device_general(playlist_items, tile_live, playlist_weights):
    masked = jnp.where(tile_live[0, 0] > 0, playlist_items, jnp.zeros_like(playlist_items))
    column = lax.all_gather(masked, "row", axis=0, tiled=True)
    weights = lax.all_gather(playlist_weights, "row", axis=0, tiled=True)
    scaled = (weights[:, None].astype(jnp.float32) * column.astype(jnp.float32)).astype(jnp.bfloat16)
    band = broadcast(column, "col", lax.axis_index("row"))
    summed = lax.dot_general(band, scaled, (((0,), (0,)), ((), ())), preferred_element_type=jnp.float32)
    return summed / jnp.float32(column.shape[0])


def pairs(*rules):
    out = []
    for n in range(32):
        at = (n >> 4, (n >> 3) & 1, (n >> 1) & 3, n & 1)
        for rule in rules:
            to = rule(*at)
            if to is not None:
                out.append((n, to[0] * 16 + to[1] * 8 + to[2] * 2 + to[3]))
    return out


def across(y, x, z, k):
    return (y, k, z, x) if z < 2 else None


def one_up(y, x, z, k):
    return (y, x, z + 1, k) if z < 2 else None


def one_to_two(y, x, z, k):
    return (y, x, 2, k) if z == 1 else None


def two_to_three(y, x, z, k):
    return (y, x, 3, k) if z == 2 else None


def one_to_none(y, x, z, k):
    return (y, x, 0, k) if z == 1 else None


ACROSS, ONE_UP, ONE_TO_TWO = pairs(across), pairs(one_up), pairs(one_to_two)
OUTWARD, TWO_TO_THREE = pairs(two_to_three, one_to_none), pairs(two_to_three)
SWAP_X = pairs(lambda y, x, z, k: (y, 1 - x, z, k))
SWAP_Y = pairs(lambda y, x, z, k: (1 - y, x, z, k))
SWAP_Z = pairs(lambda y, x, z, k: (y, x, z ^ 1, k))
CORES = pairs(lambda y, x, z, k: (y, x, z, 1 - k))


def send(value, perm):
    return lax.ppermute(value, ("row", "col"), perm)


def after(value, *others):
    return lax.optimization_barrier((value,) + others)[0]


def cuts_of(cols):
    unit = cols // 8
    at, out = 0, []
    for width in (2, 2, 2, 2):
        out.append((at, at + width * unit))
        at += width * unit
    return out


def per_device(playlist_items, tile_live, playlist_weights):
    rows, cols = playlist_items.shape
    r, c = lax.axis_index("row"), lax.axis_index("col")
    y, x, z, k = r // 2, r % 2, c // 2, c % 2
    live = tile_live[0, 0] > 0
    cuts = cuts_of(cols)

    def keep(block):
        return jnp.where(live, block, jnp.zeros_like(block))

    n = len(cuts)
    w_near = send(playlist_weights, SWAP_X)
    base = []
    for i, (lo, hi) in enumerate(cuts[:3]):
        block = keep(playlist_items[:, lo:hi])
        base.append(send(after(block, w_near) if i == 1 else block, ACROSS))
    rest = cuts[3][0]
    tail = send(keep(playlist_items[:, rest:]), ACROSS)
    base += [tail[:, lo - rest : hi - rest] for lo, hi in cuts[3:]]
    own = keep(playlist_items)
    near = send(after(own, w_near, tail), SWAP_X)

    def scale(block, weight):
        return (weight[:, None].astype(jnp.float32) * block.astype(jnp.float32)).astype(jnp.bfloat16)

    def dot(lhs, rhs):
        return lax.dot_general(lhs, rhs, (((0,), (0,)), ((), ())), preferred_element_type=jnp.float32)

    up, out, kept, given, fars = {}, {}, [], [], []

    def finish(j, *ties):
        lo, hi = cuts[j]
        high = jnp.where(z == 1, base[j], jnp.where(z == 2, up[j, 0], out[j, 0]))
        low = jnp.where(z == 0, base[j], jnp.where(z == 1, up[j, 0], up[j, 1] + out[j, 1]))
        mine = jnp.concatenate([jnp.where(y == 1, high, low), jnp.where(y == 1, low, high)], 1)
        mine = after(mine, *ties) if ties else mine
        part = dot(mine, by_mine) + dot(send(mine, CORES), by_their)
        kept.append(part[: hi - lo])
        given.append(part[hi - lo :].astype(jnp.bfloat16))
        fars.append(send(given[j], SWAP_Y))

    up[0, 0] = send(base[0], ONE_UP)
    out[0, 0] = send(jnp.where(z == 1, base[0], up[0, 0]), OUTWARD)
    up[1, 0] = send(base[1], ONE_UP)
    out[1, 0] = send(jnp.where(z == 1, base[1], up[1, 0]), OUTWARD)
    up[0, 1] = send(up[0, 0], ONE_TO_TWO)
    out[0, 1] = send(up[0, 1], TWO_TO_THREE)
    up[2, 0] = send(after(base[2], up[0, 0], out[0, 0]), ONE_UP)
    out[2, 0] = send(jnp.where(z == 1, base[2], up[2, 0]), OUTWARD)
    up[1, 1] = send(after(up[1, 0], up[1, 0], out[1, 0]), ONE_TO_TWO)
    out[1, 1] = send(up[1, 1], TWO_TO_THREE)
    up[3, 0] = send(after(base[3], up[0, 1], out[0, 1]), ONE_UP)
    out[3, 0] = send(jnp.where(z == 1, base[3], up[3, 0]), OUTWARD)
    up[2, 1] = send(after(up[2, 0], up[2, 0], out[2, 0]), ONE_TO_TWO)
    out[2, 1] = send(up[2, 1], TWO_TO_THREE)
    up[3, 1] = send(after(up[3, 0], up[1, 1], out[1, 1]), ONE_TO_TWO)
    out[3, 1] = send(up[3, 1], TWO_TO_THREE)
    here, there = scale(own, playlist_weights), scale(near, w_near)
    by_mine, by_their = jnp.where(k == x, here, there), jnp.where(k == x, there, here)
    finish(0)
    finish(1)
    finish(2, fars[0], given[1])
    finish(3, fars[1], given[2])
    sums = [a + b.astype(jnp.float32) for a, b in zip(kept, fars)]
    return jnp.concatenate(sums, 0) / jnp.float32(4 * rows)


def solution(mesh):
    tuned = mesh.shape["row"] == 4 and mesh.shape["col"] == 8
    return jax.shard_map(
        per_device if tuned else per_device_general,
        mesh=mesh,
        in_specs=(P("row", "col"), P("row", "col"), P("row")),
        out_specs=P("row", "col"),
        check_vma=False,
    )
```

```python
import jax
import jax.numpy as jnp
from jax import lax
from jax.sharding import PartitionSpec as P


def broadcast(x, axis, root):
    mine = lax.axis_index(axis) == root
    return lax.psum(jnp.where(mine, x, jnp.zeros_like(x)), axis)


def per_device_general(playlist_items, tile_live, playlist_weights):
    masked = jnp.where(tile_live[0, 0] > 0, playlist_items, jnp.zeros_like(playlist_items))
    column = lax.all_gather(masked, "row", axis=0, tiled=True)
    weights = lax.all_gather(playlist_weights, "row", axis=0, tiled=True)
    scaled = (weights[:, None].astype(jnp.float32) * column.astype(jnp.float32)).astype(jnp.bfloat16)
    band = broadcast(column, "col", lax.axis_index("row"))
    summed = lax.dot_general(band, scaled, (((0,), (0,)), ((), ())), preferred_element_type=jnp.float32)
    return summed / jnp.float32(column.shape[0])


def pairs(*rules):
    out = []
    for n in range(32):
        at = (n >> 4, (n >> 3) & 1, (n >> 1) & 3, n & 1)
        for rule in rules:
            to = rule(*at)
            if to is not None:
                out.append((n, to[0] * 16 + to[1] * 8 + to[2] * 2 + to[3]))
    return out


def across(y, x, z, k):
    return (y, k, z, x) if z < 2 else None


def one_up(y, x, z, k):
    return (y, x, z + 1, k) if z < 2 else None


def one_to_two(y, x, z, k):
    return (y, x, 2, k) if z == 1 else None


def two_to_three(y, x, z, k):
    return (y, x, 3, k) if z == 2 else None


def one_to_none(y, x, z, k):
    return (y, x, 0, k) if z == 1 else None


ACROSS, ONE_UP, ONE_TO_TWO = pairs(across), pairs(one_up), pairs(one_to_two)
OUTWARD, TWO_TO_THREE = pairs(two_to_three, one_to_none), pairs(two_to_three)
SWAP_X = pairs(lambda y, x, z, k: (y, 1 - x, z, k))
SWAP_Y = pairs(lambda y, x, z, k: (1 - y, x, z, k))
SWAP_Z = pairs(lambda y, x, z, k: (y, x, z ^ 1, k))
CORES = pairs(lambda y, x, z, k: (y, x, z, 1 - k))


def send(value, perm):
    return lax.ppermute(value, ("row", "col"), perm)


def after(value, *others):
    return lax.optimization_barrier((value,) + others)[0]


def cuts_of(cols):
    unit = cols // 8
    at, out = 0, []
    for width in (2, 2, 2, 2):
        out.append((at, at + width * unit))
        at += width * unit
    return out


def per_device(playlist_items, tile_live, playlist_weights):
    rows, cols = playlist_items.shape
    r, c = lax.axis_index("row"), lax.axis_index("col")
    y, x, z, k = r // 2, r % 2, c // 2, c % 2
    live = tile_live[0, 0] > 0
    cuts = cuts_of(cols)

    def keep(block):
        return jnp.where(live, block, jnp.zeros_like(block))

    n = len(cuts)
    w_near = send(playlist_weights, SWAP_X)
    base = []
    for i, (lo, hi) in enumerate(cuts[:3]):
        block = keep(playlist_items[:, lo:hi])
        base.append(send(after(block, w_near) if i == 1 else block, ACROSS))
    rest = cuts[3][0]
    tail = send(keep(playlist_items[:, rest:]), ACROSS)
    base += [tail[:, lo - rest : hi - rest] for lo, hi in cuts[3:]]
    own = keep(playlist_items)
    near = send(after(own, w_near, tail), SWAP_X)

    def scale(block, weight):
        return (weight[:, None].astype(jnp.float32) * block.astype(jnp.float32)).astype(jnp.bfloat16)

    def dot(lhs, rhs):
        return lax.dot_general(lhs, rhs, (((0,), (0,)), ((), ())), preferred_element_type=jnp.float32)

    up, out, kept, given, fars = {}, {}, [], [], []

    def finish(j, *ties):
        lo, hi = cuts[j]
        high = jnp.where(z == 1, base[j], jnp.where(z == 2, up[j, 0], out[j, 0]))
        low = jnp.where(z == 0, base[j], jnp.where(z == 1, up[j, 0], up[j, 1] + out[j, 1]))
        mine = jnp.concatenate([jnp.where(y == 1, high, low), jnp.where(y == 1, low, high)], 1)
        mine = after(mine, *ties) if ties else mine
        part = dot(mine, by_mine) + dot(send(mine, CORES), by_their)
        kept.append(part[: hi - lo])
        given.append(part[hi - lo :].astype(jnp.bfloat16))
        fars.append(send(given[j], SWAP_Y))

    up[0, 0] = send(base[0], ONE_UP)
    out[0, 0] = send(jnp.where(z == 1, base[0], up[0, 0]), OUTWARD)
    up[1, 0] = send(base[1], ONE_UP)
    out[1, 0] = send(jnp.where(z == 1, base[1], up[1, 0]), OUTWARD)
    up[0, 1] = send(up[0, 0], ONE_TO_TWO)
    out[0, 1] = send(up[0, 1], TWO_TO_THREE)
    up[2, 0] = send(after(base[2], up[0, 0], out[0, 0]), ONE_UP)
    out[2, 0] = send(jnp.where(z == 1, base[2], up[2, 0]), OUTWARD)
    up[1, 1] = send(after(up[1, 0], up[1, 0], out[1, 0]), ONE_TO_TWO)
    out[1, 1] = send(up[1, 1], TWO_TO_THREE)
    up[3, 0] = send(after(base[3], up[0, 1], out[0, 1]), ONE_UP)
    out[3, 0] = send(jnp.where(z == 1, base[3], up[3, 0]), OUTWARD)
    up[2, 1] = send(after(up[2, 0], up[2, 0], out[2, 0]), ONE_TO_TWO)
    out[2, 1] = send(up[2, 1], TWO_TO_THREE)
    up[3, 1] = send(after(up[3, 0], up[1, 1], out[1, 1]), ONE_TO_TWO)
    out[3, 1] = send(up[3, 1], TWO_TO_THREE)
    here, there = scale(own, playlist_weights), scale(near, w_near)
    by_mine, by_their = jnp.where(k == x, here, there), jnp.where(k == x, there, here)
    finish(0)
    finish(1)
    finish(2, fars[0], given[1])
    finish(3, fars[1], given[2])
    total = jnp.zeros((cols, cols), jnp.float32)
    for (lo, hi), mine, far in zip(cuts, kept, fars):
        total = lax.dynamic_update_slice(total, (mine + far.astype(jnp.float32)) / jnp.float32(4 * rows), (lo, 0))
    return total


def solution(mesh):
    tuned = mesh.shape["row"] == 4 and mesh.shape["col"] == 8
    return jax.shard_map(
        per_device if tuned else per_device_general,
        mesh=mesh,
        in_specs=(P("row", "col"), P("row", "col"), P("row")),
        out_specs=P("row", "col"),
        check_vma=False,
    )
```

```python
import jax
import jax.numpy as jnp
from jax import lax
from jax.sharding import PartitionSpec as P


def broadcast(x, axis, root):
    mine = lax.axis_index(axis) == root
    return lax.psum(jnp.where(mine, x, jnp.zeros_like(x)), axis)


def per_device_general(playlist_items, tile_live, playlist_weights):
    masked = jnp.where(tile_live[0, 0] > 0, playlist_items, jnp.zeros_like(playlist_items))
    column = lax.all_gather(masked, "row", axis=0, tiled=True)
    weights = lax.all_gather(playlist_weights, "row", axis=0, tiled=True)
    scaled = (weights[:, None].astype(jnp.float32) * column.astype(jnp.float32)).astype(jnp.bfloat16)
    band = broadcast(column, "col", lax.axis_index("row"))
    summed = lax.dot_general(band, scaled, (((0,), (0,)), ((), ())), preferred_element_type=jnp.float32)
    return summed / jnp.float32(column.shape[0])


def pairs(*rules):
    out = []
    for n in range(32):
        at = (n >> 4, (n >> 3) & 1, (n >> 1) & 3, n & 1)
        for rule in rules:
            to = rule(*at)
            if to is not None:
                out.append((n, to[0] * 16 + to[1] * 8 + to[2] * 2 + to[3]))
    return out


def across(y, x, z, k):
    return (y, k, z, x) if z < 2 else None


def one_up(y, x, z, k):
    return (y, x, z + 1, k) if z < 2 else None


def one_to_two(y, x, z, k):
    return (y, x, 2, k) if z == 1 else None


def two_to_three(y, x, z, k):
    return (y, x, 3, k) if z == 2 else None


def one_to_none(y, x, z, k):
    return (y, x, 0, k) if z == 1 else None


ACROSS, ONE_UP, ONE_TO_TWO = pairs(across), pairs(one_up), pairs(one_to_two)
OUTWARD, TWO_TO_THREE = pairs(two_to_three, one_to_none), pairs(two_to_three)
SWAP_X = pairs(lambda y, x, z, k: (y, 1 - x, z, k))
SWAP_Y = pairs(lambda y, x, z, k: (1 - y, x, z, k))
SWAP_Z = pairs(lambda y, x, z, k: (y, x, z ^ 1, k))
CORES = pairs(lambda y, x, z, k: (y, x, z, 1 - k))


def send(value, perm):
    return lax.ppermute(value, ("row", "col"), perm)


def after(value, *others):
    return lax.optimization_barrier((value,) + others)[0]


def cuts_of(cols):
    unit = cols // 8
    at, out = 0, []
    for width in (2, 2, 2, 2):
        out.append((at, at + width * unit))
        at += width * unit
    return out


def per_device(playlist_items, tile_live, playlist_weights):
    rows, cols = playlist_items.shape
    r, c = lax.axis_index("row"), lax.axis_index("col")
    y, x, z, k = r // 2, r % 2, c // 2, c % 2
    live = tile_live[0, 0] > 0
    cuts = cuts_of(cols)

    def keep(block):
        return jnp.where(live, block, jnp.zeros_like(block))

    n = len(cuts)
    w_near = send(playlist_weights, SWAP_X)
    base = []
    for i, (lo, hi) in enumerate(cuts[:3]):
        block = keep(playlist_items[:, lo:hi])
        base.append(send(after(block, w_near) if i == 1 else block, ACROSS))
    rest = cuts[3][0]
    tail = send(keep(playlist_items[:, rest:]), ACROSS)
    base += [tail[:, lo - rest : hi - rest] for lo, hi in cuts[3:]]
    own = keep(playlist_items)
    near = send(after(own, w_near, tail), SWAP_X)

    def scale(block, weight):
        return (weight[:, None].astype(jnp.float32) * block.astype(jnp.float32)).astype(jnp.bfloat16)

    def dot(lhs, rhs):
        return lax.dot_general(lhs, rhs, (((0,), (0,)), ((), ())), preferred_element_type=jnp.float32)

    up, out, kept, given, fars = {}, {}, [], [], []

    def finish(j, *ties):
        lo, hi = cuts[j]
        high = jnp.where(z == 1, base[j], jnp.where(z == 2, up[j, 0], out[j, 0]))
        low = jnp.where(z == 0, base[j], jnp.where(z == 1, up[j, 0], up[j, 1] + out[j, 1]))
        mine = jnp.concatenate([jnp.where(y == 1, high, low), jnp.where(y == 1, low, high)], 1)
        mine = after(mine, *ties) if ties else mine
        part = dot(mine, by_mine) + dot(send(mine, CORES), by_their)
        kept.append(part[: hi - lo])
        given.append(part[hi - lo :].astype(jnp.bfloat16))
        fars.append(send(given[j], SWAP_Y))

    up[0, 0] = send(base[0], ONE_UP)
    out[0, 0] = send(jnp.where(z == 1, base[0], up[0, 0]), OUTWARD)
    up[1, 0] = send(base[1], ONE_UP)
    out[1, 0] = send(jnp.where(z == 1, base[1], up[1, 0]), OUTWARD)
    up[0, 1] = send(up[0, 0], ONE_TO_TWO)
    out[0, 1] = send(up[0, 1], TWO_TO_THREE)
    up[2, 0] = send(after(base[2], up[0, 0], out[0, 0]), ONE_UP)
    out[2, 0] = send(jnp.where(z == 1, base[2], up[2, 0]), OUTWARD)
    up[1, 1] = send(after(up[1, 0], up[1, 0], out[1, 0]), ONE_TO_TWO)
    out[1, 1] = send(up[1, 1], TWO_TO_THREE)
    up[3, 0] = send(after(base[3], up[0, 1], out[0, 1]), ONE_UP)
    out[3, 0] = send(jnp.where(z == 1, base[3], up[3, 0]), OUTWARD)
    up[2, 1] = send(after(up[2, 0], up[2, 0], out[2, 0]), ONE_TO_TWO)
    out[2, 1] = send(up[2, 1], TWO_TO_THREE)
    up[3, 1] = send(after(up[3, 0], up[1, 1], out[1, 1]), ONE_TO_TWO)
    out[3, 1] = send(up[3, 1], TWO_TO_THREE)
    same = k == x
    by_mine = scale(jnp.where(same, own, near), jnp.where(same, playlist_weights, w_near))
    by_their = scale(jnp.where(same, near, own), jnp.where(same, w_near, playlist_weights))
    finish(0)
    finish(1)
    finish(2, fars[0], given[1])
    finish(3, fars[1], given[2])
    total = jnp.zeros((cols, cols), jnp.float32)
    for (lo, hi), mine, far in zip(cuts, kept, fars):
        total = lax.dynamic_update_slice(total, (mine + far.astype(jnp.float32)) / jnp.float32(4 * rows), (lo, 0))
    return total


def solution(mesh):
    tuned = mesh.shape["row"] == 4 and mesh.shape["col"] == 8
    return jax.shard_map(
        per_device if tuned else per_device_general,
        mesh=mesh,
        in_specs=(P("row", "col"), P("row", "col"), P("row")),
        out_specs=P("row", "col"),
        check_vma=False,
    )
```
